512 devices in a mesh: rep: 32 (over y, x_lo, core), fsdp: 16 (over x_hi, z).
Axes of the slice: x: 4 (x_hi: 2, x_lo: 2; x = x_hi * 2 + x_lo), y: 8, z: 8, core: 2. Of those that a mesh axis runs over, the one named last changes fastest.
Arguments:
- tokens: bfloat16 [32, 2048, 4096], P('rep', 'fsdp'), may hold values from -6 to 6
- cotangent: bfloat16 [32, 2048, 512], P('rep', 'fsdp'), may hold values from -6 to 6
- params: bfloat16 [32, 4096, 512], P('rep', 'fsdp'), may hold values from -0.09375 to 0.09375
- first_moment: float32 [32, 4096, 512], P('rep', 'fsdp'), may hold values from -0.12 to 0.12
- second_moment: float32 [32, 4096, 512], P('rep', 'fsdp'), may hold values from 0.0001 to 0.001
- weight: bfloat16 [32], P('rep'), may hold values from 0.5 to 2
- step: int32 [1], replicated, may hold values from 0 to 999
Outputs:
- keys: bfloat16 [32, 2048, 512], P('rep', 'fsdp')
- token_grad: bfloat16 [32, 2048, 4096], P('rep', 'fsdp')
- new_params: bfloat16 [32, 4096, 512], P('rep', 'fsdp')
- new_first: float32 [32, 4096, 512], P('rep', 'fsdp')
- new_second: float32 [32, 4096, 512], P('rep', 'fsdp')
- new_weight: float32 [32], P('rep')
The draws below stay inside these ranges and needn't reach their ends.
All inputs are finite; a program needn't handle non-finite values.
Results may differ from the reference program's by a relative error of at most 0.008.
Values may be sent and summed in bfloat16 or wider, within the bound.
No kernel may reach another device: no remote copies, remote signals or barrier semaphores. Data moves between devices by JAX's collectives and lax.ppermute only.
A program may use at most 64 MiB of HBM per device.

```python
import math
import jax
import jax.numpy as jnp
from jax import lax

D = 4096
TOK_DEV = 128
KW = 512
TOKENS = 2048
N_REP = 32
N_FSDP = 16


def levels(own_key, shape, split, least, high):
    level, own = 1.0, jax.random.fold_in(own_key, 6)
    for position, parts in split:
        draws = jnp.exp(jax.random.uniform(jax.random.fold_in(own, position), (parts,), jnp.float32, least / len(split), high / len(split)))
        level = level * jnp.repeat(draws, shape[position] // parts).reshape([-1 if axis == position else 1 for axis in range(len(shape))])
    return level


def scatter_about(stream_key, extent, scale, reach, cuts=(), kind=jnp.bfloat16):
    result = scale * jax.random.normal(stream_key, extent, jnp.float32)
    if cuts:
        result = result * levels(stream_key, extent, cuts, -0.22, 0.18)
    return jnp.clip(result, -reach, reach).astype(kind)


def setup_inputs(seed: int = 0) -> dict:
    arg_keys = jax.random.split(jax.random.key(seed), 8)
    tokens = scatter_about(arg_keys[0], (N_REP, TOKENS, D), 1.0, 6.0, ((0, 32), (1, 16)))
    cotangent = scatter_about(arg_keys[1], (N_REP, TOKENS, KW), 1.0, 6.0, ((0, 32), (1, 16)))
    params = scatter_about(arg_keys[2], (N_REP, D, KW), D ** -0.5, 0.09375, ((0, 32), (1, 16)))
    first_moment = scatter_about(arg_keys[3], (N_REP, D, KW), 0.02, 0.12, ((0, 32), (1, 16)), jnp.float32)
    second_moment = jnp.clip(jnp.exp(math.log(0.001) - 2.3025852 * jax.random.uniform(arg_keys[4], (N_REP, D, KW), jnp.float32) ** levels(arg_keys[4], (N_REP, D, KW), ((0, 32), (1, 16)), -0.2, 0.2)), 0.0001, 0.001)
    weight = jnp.clip(jnp.exp(math.log(2.0) - 1.3862944 * jax.random.uniform(arg_keys[5], (N_REP,), jnp.float32) ** levels(arg_keys[5], (N_REP,), ((0, 32),), -0.2, 0.2)), 0.5, 2.0).astype(jnp.bfloat16)
    step = jax.random.randint(arg_keys[6], (1,), 0, 1000).astype(jnp.int32)
    return dict(tokens=tokens, cotangent=cotangent, params=params, first_moment=first_moment, second_moment=second_moment, weight=weight, step=step)


LEARN = 0.002
BETA_ONE = 0.9
BETA_TWO = 0.999
EPSILON = 1e-08

def reference(tokens, cotangent, params, first_moment, second_moment, weight, step):
    tstep = step[0]
    count = (tstep + 1).astype(jnp.float32)
    bias_one = 1.0 - jnp.power(jnp.float32(BETA_ONE), count)
    bias_two = 1.0 - jnp.power(jnp.float32(BETA_TWO), count)

    def one_group(items):
        tok_rows, cot_rows, numer, moment_one, moment_two, mass = items
        debiased = (numer.astype(jnp.float32) / mass.astype(jnp.float32)).astype(jnp.bfloat16)
        keys = jnp.dot(tok_rows, debiased, preferred_element_type=jnp.float32).astype(jnp.bfloat16)
        token_grad = jnp.dot(cot_rows, debiased.T, preferred_element_type=jnp.float32).astype(jnp.bfloat16)
        tok_blocks = tok_rows.reshape(N_FSDP, TOK_DEV, D).astype(jnp.float32)
        cot_blocks = cot_rows.reshape(N_FSDP, TOK_DEV, KW).astype(jnp.float32)
        partial_terms = jnp.einsum('ntd,ntk->ndk', tok_blocks, cot_blocks).astype(jnp.bfloat16)
        partial_terms = lax.optimization_barrier(partial_terms)
        grad = lax.optimization_barrier(jnp.sum(partial_terms.astype(jnp.float32), axis=0)) / jnp.float32(TOKENS)
        new_first = BETA_ONE * moment_one + (1.0 - BETA_ONE) * grad
        new_second = BETA_TWO * moment_two + (1.0 - BETA_TWO) * grad * grad
        update = LEARN * (new_first / bias_one) / (jnp.sqrt(new_second / bias_two) + EPSILON)
        outgoing = (numer.astype(jnp.float32) - update).astype(jnp.bfloat16)
        return (keys, token_grad, outgoing, new_first, new_second)
    keys, token_grad, outgoing, new_first, new_second = lax.map(one_group, (tokens, cotangent, params, first_moment, second_moment, weight))
    distance = jnp.left_shift(jnp.int32(1), tstep % 4) % N_REP
    incoming = jnp.roll(outgoing, distance, axis=0)
    new_params = ((outgoing.astype(jnp.float32) + incoming.astype(jnp.float32)) * 0.5).astype(jnp.bfloat16)
    mass = weight.astype(jnp.float32)
    new_weight = (mass + jnp.roll(mass, distance, axis=0)) * 0.5
    return (keys, token_grad, new_params, new_first, new_second, new_weight)
```

```python
from functools import partial

import jax
import jax.numpy as jnp
from jax import lax
from jax.sharding import Mesh, PartitionSpec as P

LEARN = 0.002
BETA_ONE = 0.9
BETA_TWO = 0.999
EPSILON = 1e-08
GROUP = ("xh", "zq", "zp")
REPS = ("y", "xl", "c")
PAIRS = ("c", "xh", "zq", "zp")


def feature_groups():
    groups = []
    for core in range(2):
        for k in range(4):
            even = 2 * k if core == 0 else (2 * k + 2) % 8
            odd = 2 * k + 1
            groups.append([core * 16 + xh * 8 + z for xh in range(2) for z in (even, odd)])
    return groups


def swap_features(x):
    return lax.all_to_all(x, PAIRS, 0, 0, axis_index_groups=feature_groups(), tiled=True)


def swap_tokens(x):
    return lax.all_to_all(x, "zq", 0, 0, tiled=True)


def pushed(outgoing, hop):
    pairs = [(source, (source + hop) % 32) for source in range(32)]
    return lax.ppermute(outgoing, REPS, pairs)


def body(tokens, cotangent, params, first_moment, second_moment, weight, step):
    numer = params[0].astype(jnp.float32)
    mass = weight.astype(jnp.float32)[0]
    debiased = (numer / mass).astype(jnp.bfloat16)
    rows = swap_tokens(jnp.broadcast_to(debiased, (4, 256, 512))).reshape(1024, 512)

    columns = tokens[0].reshape(128, 2, 4, 2, 256).transpose(1, 3, 0, 2, 4).reshape(4, 128, 1024)
    out = jnp.concatenate([columns, jnp.broadcast_to(cotangent[0], (4, 128, 512))], axis=2)
    got = swap_features(out).reshape(512, 1536)
    tok, cot = got[:, :1024], got[:, 1024:]

    share = lax.dot_general(tok, cot, (((0,), (0,)), ((), ())), preferred_element_type=jnp.float32)
    shares = swap_tokens(share.astype(jnp.bfloat16).reshape(4, 256, 512))

    keys = jnp.dot(tok, rows, preferred_element_type=jnp.float32).astype(jnp.bfloat16)
    token_grad = lax.dot_general(
        cot, rows, (((1,), (1,)), ((), ())), preferred_element_type=jnp.float32
    ).astype(jnp.bfloat16)
    back = swap_features(
        jnp.concatenate([token_grad, keys], axis=1).reshape(4, 128, 1536)
    )
    keys = back[:, :, 1024:].astype(jnp.float32).sum(axis=0).astype(jnp.bfloat16)
    token_grad = (
        back[:, :, :1024].reshape(2, 2, 128, 4, 256).transpose(2, 0, 3, 1, 4).reshape(128, 4096)
    )

    grad = shares.astype(jnp.float32).sum(axis=0) / jnp.float32(2048)
    tstep = step[0]
    count = (tstep + 1).astype(jnp.float32)
    bias_one = 1.0 - jnp.power(jnp.float32(BETA_ONE), count)
    bias_two = 1.0 - jnp.power(jnp.float32(BETA_TWO), count)
    new_first = BETA_ONE * first_moment[0] + (1.0 - BETA_ONE) * grad
    new_second = BETA_TWO * second_moment[0] + (1.0 - BETA_TWO) * grad * grad
    update = LEARN * (new_first / bias_one) / (jnp.sqrt(new_second / bias_two) + EPSILON)
    outgoing = (numer - update).astype(jnp.bfloat16)
    sent = jnp.concatenate([outgoing, jnp.broadcast_to(weight[0], (16, 512))], axis=0)
    branches = [partial(pushed, hop=2**level) for level in range(4)]
    incoming = lax.switch(tstep % 4, branches, sent)
    new_params = (
        (outgoing.astype(jnp.float32) + incoming[:256].astype(jnp.float32)) * 0.5
    ).astype(jnp.bfloat16)
    new_weight = (weight.astype(jnp.float32) + incoming[256, :1].astype(jnp.float32)) * 0.5
    return (
        keys[None],
        token_grad[None],
        new_params[None],
        new_first[None],
        new_second[None],
        new_weight,
    )


def solution(mesh):
    fine = Mesh(mesh.devices.reshape(8, 2, 2, 2, 4, 2), REPS + GROUP)
    rows = P(REPS, GROUP, None)
    return jax.shard_map(
        body,
        mesh=fine,
        in_specs=(rows, rows, rows, rows, rows, P(REPS), P()),
        out_specs=(rows, rows, rows, rows, rows, P(REPS)),
        check_vma=False,
    )
```

```python
from functools import partial

import jax
import jax.numpy as jnp
from jax import lax
from jax.experimental import pallas as pl
from jax.experimental.pallas import tpu as pltpu
from jax.sharding import Mesh, PartitionSpec as P

LEARN = 0.002
BETA_ONE = 0.9
BETA_TWO = 0.999
EPSILON = 1e-08
GROUP = ("xh", "zq", "zp")
REPS = ("y", "xl", "c")
PAIRS = ("c", "xh", "zq", "zp")
F32 = jnp.float32
BF16 = jnp.bfloat16


def neighbour(core, z):
    return z ^ 1 if core == 0 else ((z + 1) ^ 1) - 1 & 7


def feature_groups():
    groups = []
    for core in range(2):
        for even in range(0, 8, 2):
            zs = (even, neighbour(core, even))
            groups.append([core * 16 + xh * 8 + z for xh in range(2) for z in zs])
    return groups


def partner_pairs(relative):
    pairs = []
    for core in range(2):
        for xh in range(2):
            for z in range(8):
                to_z = neighbour(core, z) if relative & 1 else z
                to_x = xh ^ (relative >> 1)
                pairs.append((core * 16 + xh * 8 + z, core * 16 + to_x * 8 + to_z))
    return pairs


def along_quad(x, step):
    return lax.ppermute(x, "zq", [(i, (i + step) % 4) for i in range(4)])


def pushed(outgoing, hop):
    pairs = [(source, (source + hop) % 32) for source in range(32)]
    return lax.ppermute(outgoing, REPS, pairs)


VMEM = pl.BlockSpec(memory_space=pltpu.VMEM)
ANY = pl.BlockSpec(memory_space=pl.ANY)
SMEM = pl.BlockSpec(memory_space=pltpu.SMEM)


def params_of(flops=0, moved=0, mib=48):
    return dict(
        compiler_params=pltpu.CompilerParams(vmem_limit_bytes=mib << 20),
        cost_estimate=pl.CostEstimate(flops=flops, bytes_accessed=moved, transcendentals=0),
    )


def pack_kernel(t0, t1, t2, t3, cot, out):
    for q, part in enumerate((t0, t1, t2, t3)):
        out[0, :, q * 256 : (q + 1) * 256] = part[...]
    out[0, :, 1024:] = cot[...]


def pack(tokens, cot):
    columns = [
        pl.BlockSpec((128, 256), lambda c, q=q: (0, (c // 2) * 8 + q * 2 + c % 2)) for q in range(4)
    ]
    return pl.pallas_call(
        pack_kernel,
        grid=(4,),
        in_specs=[*columns, pl.BlockSpec((128, 512), lambda c: (0, 0))],
        out_specs=pl.BlockSpec((1, 128, 1536), lambda c: (c, 0, 0)),
        out_shape=pltpu.HBM((4, 128, 1536), BF16),
        name="pack",
        **params_of(0, 3 << 20),
    )(tokens, tokens, tokens, tokens, cot)


def share_kernel(tok, cot, out):
    out[0] = lax.dot_general(
        tok[...], cot[...], (((0,), (0,)), ((), ())), preferred_element_type=F32
    ).astype(BF16)


def share(got):
    return pl.pallas_call(
        share_kernel,
        grid=(4,),
        in_specs=[pl.BlockSpec((512, 256), lambda q: (0, q)), pl.BlockSpec((512, 512), lambda q: (0, 2))],
        out_specs=pl.BlockSpec((1, 256, 512), lambda q: (q, 0, 0)),
        out_shape=pltpu.HBM((4, 256, 512), BF16),
        name="share",
        **params_of(2 * 512 * 1024 * 512, 5 << 19),
    )(got, got)


def product_kernel(got, own_w, w_down, w_up, far_a, far_b, own, to_z, to_x, to_xz, total):
    place = lax.axis_index("xh") * 2 + lax.axis_index("zp")
    quad = lax.axis_index("zq")
    cot = got[:, 1024:]
    keys = None
    for k, w in enumerate((own_w, w_up, None, w_down)):
        w = jnp.concatenate([far_a[...], far_b[...]], axis=0) if w is None else w[...]
        columns = pl.ds(pl.multiple_of(lax.rem(quad + k, 4) * 256, 256), 256)
        term = jnp.dot(got[:, columns], w, preferred_element_type=F32)
        keys = term if keys is None else keys + term
        total[:, columns] = lax.dot_general(
            cot, w, (((1,), (1,)), ((), ())), preferred_element_type=F32
        ).astype(BF16)
    total[:, 1024:] = keys.astype(BF16)
    for relative, out in enumerate((own, to_z, to_x, to_xz)):
        rows = pl.ds(pl.multiple_of((place ^ relative) * 128, 128), 128)
        out[...] = total[rows, :]


def products(got, own_w, w_down, w_up, far_a, far_b):
    block = jax.ShapeDtypeStruct((128, 1536), BF16)
    return pl.pallas_call(
        product_kernel,
        in_specs=[VMEM] * 6,
        out_specs=[VMEM] * 4,
        out_shape=[block] * 4,
        scratch_shapes=[pltpu.VMEM((512, 1536), BF16)],
        name="products",
        **params_of(4 * 512 * 1024 * 512, 4 << 20),
    )(got, own_w, w_down, w_up, far_a, far_b)


def adam_kernel(weight, bias, shares, first, second, numer, new_first, new_second, sent):
    total = shares[0].astype(F32)
    for q in range(1, 4):
        total = total + shares[q].astype(F32)
    grad = total / 2048.0
    one = BETA_ONE * first[...] + (1.0 - BETA_ONE) * grad
    two = BETA_TWO * second[...] + (1.0 - BETA_TWO) * grad * grad
    new_first[...] = one
    new_second[...] = two
    update = LEARN * (one / bias[0]) / (jnp.sqrt(two / bias[1]) + EPSILON)
    sent[:256, :] = (numer[...].astype(F32) - update).astype(BF16)
    sent[256:, :] = jnp.full((16, 512), weight[0], F32).astype(BF16)


def adam(weight, bias, shares, first, second, numer):
    state = jax.ShapeDtypeStruct((256, 512), F32)
    return pl.pallas_call(
        adam_kernel,
        in_specs=[SMEM, SMEM] + [VMEM] * 4,
        out_specs=[VMEM] * 3,
        out_shape=[state, state, jax.ShapeDtypeStruct((272, 512), BF16)],
        name="adam",
        **params_of(0, 4 << 20),
    )(weight, bias, shares, first, second, numer)


def finish_kernel(sent, incoming, own, from_z, from_x, from_xz, new_params, mixed, token_grad, keys):
    new_params[...] = (
        (sent[:256, :].astype(F32) + incoming[:256, :].astype(F32)) * 0.5
    ).astype(BF16)
    mixed[0] = (jnp.max(sent[256:264, :128].astype(F32)) + jnp.max(incoming[256:264, :128].astype(F32))) * 0.5
    place = lax.axis_index("xh") * 2 + lax.axis_index("zp")
    total = None
    for relative, part in enumerate((own, from_z, from_x, from_xz)):
        cls = place ^ relative
        for q in range(4):
            column = (cls // 2) * 2048 + q * 512 + (cls % 2) * 256
            token_grad[:, pl.ds(pl.multiple_of(column, 256), 256)] = part[:, q * 256 : (q + 1) * 256]
        term = part[:, 1024:].astype(F32)
        total = term if total is None else total + term
    keys[...] = total.astype(BF16)


def finish(sent, incoming, own, from_z, from_x, from_xz):
    return pl.pallas_call(
        finish_kernel,
        in_specs=[VMEM] * 6,
        out_specs=[VMEM, SMEM, VMEM, VMEM],
        out_shape=[
            jax.ShapeDtypeStruct((256, 512), BF16),
            jax.ShapeDtypeStruct((1,), F32),
            jax.ShapeDtypeStruct((128, 4096), BF16),
            jax.ShapeDtypeStruct((128, 512), BF16),
        ],
        name="finish",
        **params_of(0, 4 << 20),
    )(sent, incoming, own, from_z, from_x, from_xz)


def step_with(tokens, cotangent, params, first_moment, second_moment, weight, step, hop):
    mass = weight.astype(F32)
    tstep = step[0]
    count = (tstep + 1).astype(F32)
    bias = 1.0 - jnp.power(jnp.array([BETA_ONE, BETA_TWO], F32), count)

    debiased = (params[0].astype(F32) / mass[0]).astype(BF16)
    out = pack(tokens[0], cotangent[0])
    w_down = along_quad(debiased, 1)
    w_up = along_quad(debiased, -1)
    got = lax.all_to_all(out, PAIRS, 0, 0, axis_index_groups=feature_groups(), tiled=True)
    far_a = along_quad(w_down[:128], 1)
    far_b = along_quad(w_up[128:], -1)
    got, far_a, far_b = lax.optimization_barrier((got.reshape(512, 1536), far_a, far_b))

    shares = lax.all_to_all(share(got), "zq", 0, 0, tiled=True)

    own, *sends = products(got, debiased, w_down, w_up, far_a, far_b)
    back = [lax.ppermute(x, PAIRS, partner_pairs(r + 1)) for r, x in enumerate(sends)]

    new_first, new_second, sent = adam(
        mass, bias, shares, first_moment[0], second_moment[0], params[0]
    )
    incoming = pushed(sent, hop)
    new_params, mixed, token_grad, keys = finish(sent, incoming, own, *back)
    return (
        keys[None],
        token_grad[None],
        new_params[None],
        new_first[None],
        new_second[None],
        mixed,
    )


def body(*args):
    branches = [partial(step_with, hop=2**level) for level in range(4)]
    return lax.switch(args[-1][0] & 3, branches, *args)


def solution(mesh):
    fine = Mesh(mesh.devices.reshape(8, 2, 2, 2, 4, 2), REPS + GROUP)
    rows = P(REPS, GROUP, None)
    return jax.shard_map(
        body,
        mesh=fine,
        in_specs=(rows, rows, rows, rows, rows, P(REPS), P()),
        out_specs=(rows, rows, rows, rows, rows, P(REPS)),
        check_vma=False,
    )
```

```python
from functools import partial

import jax
import jax.numpy as jnp
from jax import lax
from jax.experimental import pallas as pl
from jax.experimental.pallas import tpu as pltpu
from jax.sharding import Mesh, PartitionSpec as P

LEARN = 0.002
BETA_ONE = 0.9
BETA_TWO = 0.999
EPSILON = 1e-08
GROUP = ("xh", "zq", "zp")
REPS = ("y", "xl", "c")
PAIRS = ("c", "xh", "zq", "zp")
SHARE = 64 << 20
ADAM = 64 << 20
COMBINE = 64 << 20
F32 = jnp.float32
BF16 = jnp.bfloat16


def neighbour(core, z):
    return z ^ 1 if core == 0 else ((z + 1) ^ 1) - 1 & 7


def partner_pairs(relative):
    pairs = []
    for core in range(2):
        for xh in range(2):
            for z in range(8):
                to_z = neighbour(core, z) if relative & 1 else z
                to_x = xh ^ (relative >> 1)
                pairs.append((core * 16 + xh * 8 + z, core * 16 + to_x * 8 + to_z))
    return pairs


def along_quad(x, step):
    return lax.ppermute(x, "zq", [(i, (i + step) % 4) for i in range(4)])


def swap_tokens(x):
    return lax.all_to_all(x, "zq", 0, 0, tiled=True)


def swap_features(x, relative):
    return lax.ppermute(x, PAIRS, partner_pairs(relative))


def pushed(outgoing, hop):
    pairs = [(source, (source + hop) % 32) for source in range(32)]
    return lax.ppermute(outgoing, REPS, pairs)


VMEM = pl.BlockSpec(memory_space=pltpu.VMEM)
ANY = pl.BlockSpec(memory_space=pl.ANY)
SMEM = pl.BlockSpec(memory_space=pltpu.SMEM)


def params_of(flops=0, moved=0, mib=48):
    return dict(
        compiler_params=pltpu.CompilerParams(vmem_limit_bytes=mib << 20),
        cost_estimate=pl.CostEstimate(flops=flops, bytes_accessed=moved, transcendentals=0),
    )


def pack_kernel(tokens, cot, own, to_z, to_x, to_xz):
    place = lax.axis_index("xh") * 2 + lax.axis_index("zp")
    for relative, out in enumerate((own, to_z, to_x, to_xz)):
        cls = place ^ relative
        for q in range(4):
            column = (cls // 2) * 2048 + q * 512 + (cls % 2) * 256
            out[:, q * 256 : (q + 1) * 256] = tokens[:, pl.ds(pl.multiple_of(column, 256), 256)]
        out[:, 1024:] = cot[...]


def pack(tokens, cot):
    return pl.pallas_call(
        pack_kernel,
        in_specs=[VMEM] * 2,
        out_specs=[VMEM] * 4,
        out_shape=[jax.ShapeDtypeStruct((128, 1536), BF16)] * 4,
        name="pack",
        **params_of(0, 3 << 20),
    )(tokens, cot)


def share_kernel(t0, t1, t2, t3, c0, c1, c2, c3, out):
    total = None
    for tok, cot in ((t0, c0), (t1, c1), (t2, c2), (t3, c3)):
        term = lax.dot_general(
            tok[...], cot[...], (((0,), (0,)), ((), ())), preferred_element_type=F32
        )
        total = term if total is None else total + term
    out[0] = total.astype(BF16)


def share(blocks):
    return pl.pallas_call(
        share_kernel,
        grid=(4,),
        in_specs=[pl.BlockSpec((128, 256), lambda q: (0, q))] * 4
        + [pl.BlockSpec((128, 512), lambda q: (0, 2))] * 4,
        out_specs=pl.BlockSpec((1, 256, 512), lambda q: (q, 0, 0)),
        out_shape=pltpu.HBM((4, 256, 512), BF16),
        name="share",
        **params_of(0, SHARE),
    )(*blocks, *blocks)


def product_kernel(b0, b1, b2, b3, w0, w1, w2, w3, own, to_z, to_x, to_xz, got):
    quad = lax.axis_index("zq")
    for k, block in enumerate((b0, b1, b2, b3)):
        got[k * 128 : (k + 1) * 128, :] = block[...]
    outs = (own, to_z, to_x, to_xz)
    cot = got[:, 1024:]
    keys = None
    for q, w in enumerate((w0, w1, w2, w3)):
        columns = pl.ds(pl.multiple_of(lax.rem(quad + q, 4) * 256, 256), 256)
        term = jnp.dot(got[:, columns], w[...], preferred_element_type=F32)
        keys = term if keys is None else keys + term
        part = lax.dot_general(
            cot, w[...], (((1,), (1,)), ((), ())), preferred_element_type=F32
        ).astype(BF16)
        for k, out in enumerate(outs):
            out[:, columns] = part[k * 128 : (k + 1) * 128, :]
    keys = keys.astype(BF16)
    for k, out in enumerate(outs):
        out[:, 1024:] = keys[k * 128 : (k + 1) * 128, :]


def products(blocks, w):
    block = jax.ShapeDtypeStruct((128, 1536), BF16)
    return pl.pallas_call(
        product_kernel,
        in_specs=[VMEM] * 8,
        out_specs=[VMEM] * 4,
        out_shape=[block] * 4,
        scratch_shapes=[pltpu.VMEM((512, 1536), BF16)],
        name="products",
        **params_of(4 * 512 * 1024 * 512, 4 << 20),
    )(*blocks, *w)


def adam_kernel(weight, bias, shares, first, second, numer, new_first, new_second, sent):
    total = shares[0].astype(F32)
    for q in range(1, 4):
        total = total + shares[q].astype(F32)
    grad = total / 2048.0
    one = BETA_ONE * first[...] + (1.0 - BETA_ONE) * grad
    two = BETA_TWO * second[...] + (1.0 - BETA_TWO) * grad * grad
    new_first[...] = one
    new_second[...] = two
    update = LEARN * (one / bias[0]) / (jnp.sqrt(two / bias[1]) + EPSILON)
    sent[:256, :] = (numer[...].astype(F32) - update).astype(BF16)
    sent[256:, :] = jnp.full((16, 512), weight[0], F32).astype(BF16)


def adam(weight, bias, shares, first, second, numer):
    state = jax.ShapeDtypeStruct((256, 512), F32)
    return pl.pallas_call(
        adam_kernel,
        in_specs=[SMEM, SMEM] + [VMEM] * 4,
        out_specs=[VMEM] * 3,
        out_shape=[state, state, jax.ShapeDtypeStruct((272, 512), BF16)],
        name="adam",
        **params_of(0, ADAM),
    )(weight, bias, shares, first, second, numer)


def combine_kernel(sent, incoming, new_params, mixed):
    new_params[...] = (
        (sent[:256, :].astype(F32) + incoming[:256, :].astype(F32)) * 0.5
    ).astype(BF16)
    mixed[0] = (
        jnp.max(sent[256:264, :128].astype(F32)) + jnp.max(incoming[256:264, :128].astype(F32))
    ) * 0.5


def combine(sent, incoming):
    return pl.pallas_call(
        combine_kernel,
        in_specs=[VMEM] * 2,
        out_specs=[VMEM, SMEM],
        out_shape=[jax.ShapeDtypeStruct((256, 512), BF16), jax.ShapeDtypeStruct((1,), F32)],
        name="combine",
        **params_of(0, COMBINE),
    )(sent, incoming)


def unpack_kernel(own, from_z, from_x, from_xz, token_grad, keys):
    place = lax.axis_index("xh") * 2 + lax.axis_index("zp")
    total = None
    for relative, part in enumerate((own, from_z, from_x, from_xz)):
        cls = place ^ relative
        for q in range(4):
            column = (cls // 2) * 2048 + q * 512 + (cls % 2) * 256
            token_grad[:, pl.ds(pl.multiple_of(column, 256), 256)] = part[:, q * 256 : (q + 1) * 256]
        term = part[:, 1024:].astype(F32)
        total = term if total is None else total + term
    keys[...] = total.astype(BF16)


def unpack(own, from_z, from_x, from_xz):
    return pl.pallas_call(
        unpack_kernel,
        in_specs=[VMEM] * 4,
        out_specs=[VMEM] * 2,
        out_shape=[jax.ShapeDtypeStruct((128, 4096), BF16), jax.ShapeDtypeStruct((128, 512), BF16)],
        name="unpack",
        **params_of(0, 3 << 20),
    )(own, from_z, from_x, from_xz)


def step_with(tokens, cotangent, params, first_moment, second_moment, weight, step, hop):
    mass = weight.astype(F32)
    tstep = step[0]
    count = (tstep + 1).astype(F32)
    bias = 1.0 - jnp.power(jnp.array([BETA_ONE, BETA_TWO], F32), count)

    debiased = (params[0].astype(F32) / mass[0]).astype(BF16)
    w_down = along_quad(debiased, 1)
    w_up = along_quad(debiased, -1)
    far = jnp.concatenate([along_quad(w_down[:128], 1), along_quad(w_up[128:], -1)], axis=0)
    rows = [debiased, w_up, far, w_down]
    own, *sends = pack(tokens[0], cotangent[0])
    blocks = [own] + [swap_features(x, r + 1) for r, x in enumerate(sends)]
    rows, blocks = lax.optimization_barrier((rows, blocks))
    shares = swap_tokens(share(blocks))

    own, *sends = products(blocks, rows)
    back = [swap_features(x, r + 1) for r, x in enumerate(sends)]

    new_first, new_second, sent = adam(
        mass, bias, shares, first_moment[0], second_moment[0], params[0]
    )
    incoming = pushed(sent, hop)
    new_params, mixed = combine(sent, incoming)
    token_grad, keys = unpack(own, *back)
    return (
        keys[None],
        token_grad[None],
        new_params[None],
        new_first[None],
        new_second[None],
        mixed,
    )


def body(*args):
    branches = [partial(step_with, hop=2**level) for level in range(4)]
    return lax.switch(args[-1][0] & 3, branches, *args)


def solution(mesh):
    fine = Mesh(mesh.devices.reshape(8, 2, 2, 2, 4, 2), REPS + GROUP)
    rows = P(REPS, GROUP, None)
    return jax.shard_map(
        body,
        mesh=fine,
        in_specs=(rows, rows, rows, rows, rows, P(REPS), P()),
        out_specs=(rows, rows, rows, rows, rows, P(REPS)),
        check_vma=False,
    )
```

```python
from functools import partial

import jax
import jax.numpy as jnp
from jax import lax
from jax.experimental import pallas as pl
from jax.experimental.pallas import tpu as pltpu
from jax.sharding import Mesh, PartitionSpec as P

LEARN = 0.002
BETA_ONE = 0.9
BETA_TWO = 0.999
EPSILON = 1e-08
GROUP = ("xh", "zq", "zp")
REPS = ("y", "xl", "c")
PAIRS = ("c", "xh", "zq", "zp")
SHARE = 64 << 20
ADAM = 64 << 20
COMBINE = 64 << 20
F32 = jnp.float32
BF16 = jnp.bfloat16


def neighbour(core, z):
    return z ^ 1 if core == 0 else ((z + 1) ^ 1) - 1 & 7


def partner_pairs(relative):
    pairs = []
    for core in range(2):
        for xh in range(2):
            for z in range(8):
                to_z = neighbour(core, z) if relative & 1 else z
                to_x = xh ^ (relative >> 1)
                pairs.append((core * 16 + xh * 8 + z, core * 16 + to_x * 8 + to_z))
    return pairs


def along_quad(x, step):
    return lax.ppermute(x, "zq", [(i, (i + step) % 4) for i in range(4)])


def swap_tokens(x):
    return lax.all_to_all(x, "zq", 0, 0, tiled=True)


def swap_features(x, relative):
    return lax.ppermute(x, PAIRS, partner_pairs(relative))


def pushed(outgoing, hop):
    pairs = [(source, (source + hop) % 32) for source in range(32)]
    return lax.ppermute(outgoing, REPS, pairs)


VMEM = pl.BlockSpec(memory_space=pltpu.VMEM)
ANY = pl.BlockSpec(memory_space=pl.ANY)
SMEM = pl.BlockSpec(memory_space=pltpu.SMEM)


def params_of(flops=0, moved=0, mib=24):
    return dict(
        compiler_params=pltpu.CompilerParams(vmem_limit_bytes=mib << 20),
        cost_estimate=pl.CostEstimate(flops=flops, bytes_accessed=moved, transcendentals=0),
    )


def pack_kernel(tokens, cot, own, to_z, to_x, to_xz):
    place = lax.axis_index("xh") * 2 + lax.axis_index("zp")
    for relative, out in enumerate((own, to_z, to_x, to_xz)):
        cls = place ^ relative
        for q in range(4):
            column = (cls // 2) * 2048 + q * 512 + (cls % 2) * 256
            out[:, q * 256 : (q + 1) * 256] = tokens[:, pl.ds(pl.multiple_of(column, 256), 256)]
        out[:, 1024:] = cot[...]


def pack(tokens, cot):
    return pl.pallas_call(
        pack_kernel,
        in_specs=[VMEM] * 2,
        out_specs=[VMEM] * 4,
        out_shape=[jax.ShapeDtypeStruct((128, 1536), BF16)] * 4,
        name="pack",
        **params_of(0, 3 << 20),
    )(tokens, cot)


def share_kernel(b0, b1, b2, b3, out, total, sems):
    copies = []
    for q in range(4):
        columns = slice(q * 256, (q + 1) * 256)
        part = None
        for block in (b0, b1, b2, b3):
            term = lax.dot_general(
                block[:, columns], block[:, 1024:], (((0,), (0,)), ((), ())), preferred_element_type=F32
            )
            part = term if part is None else part + term
        total[q] = part.astype(BF16)
        copy = pltpu.make_async_copy(total.at[q], out.at[q], sems.at[q])
        copy.start()
        copies.append(copy)
    for copy in copies:
        copy.wait()


def share(blocks):
    return pl.pallas_call(
        share_kernel,
        in_specs=[VMEM] * 4,
        out_specs=ANY,
        out_shape=pltpu.HBM((4, 256, 512), BF16),
        scratch_shapes=[pltpu.VMEM((4, 256, 512), BF16), pltpu.SemaphoreType.DMA((4,))],
        name="share",
        **params_of(2 * 512 * 1024 * 512, 3 << 20),
    )(*blocks)


def product_kernel(weight, b0, b1, b2, b3, w0, w1, w2, w3, own, to_z, to_x, to_xz, got):
    quad = lax.axis_index("zq")
    for k, block in enumerate((b0, b1, b2, b3)):
        got[k * 128 : (k + 1) * 128, :] = block[...]
    outs = (own, to_z, to_x, to_xz)
    cot = got[:, 1024:]
    keys = None
    for q, w in enumerate((w0, w1, w2, w3)):
        columns = pl.ds(pl.multiple_of(lax.rem(quad + q, 4) * 256, 256), 256)
        w = (w[...].astype(F32) / weight[0]).astype(BF16)
        term = jnp.dot(got[:, columns], w, preferred_element_type=F32)
        keys = term if keys is None else keys + term
        part = lax.dot_general(
            cot, w, (((1,), (1,)), ((), ())), preferred_element_type=F32
        ).astype(BF16)
        for k, out in enumerate(outs):
            out[:, columns] = part[k * 128 : (k + 1) * 128, :]
    keys = keys.astype(BF16)
    for k, out in enumerate(outs):
        out[:, 1024:] = keys[k * 128 : (k + 1) * 128, :]


def products(weight, blocks, w):
    block = jax.ShapeDtypeStruct((128, 1536), BF16)
    return pl.pallas_call(
        product_kernel,
        in_specs=[SMEM] + [VMEM] * 8,
        out_specs=[VMEM] * 4,
        out_shape=[block] * 4,
        scratch_shapes=[pltpu.VMEM((512, 1536), BF16)],
        name="products",
        **params_of(4 * 512 * 1024 * 512, 4 << 20),
    )(weight, *blocks, *w)


def stage_kernel(first, second, numer, first_out, second_out, numer_out):
    first_out[...] = first[...]
    second_out[...] = second[...]
    numer_out[...] = numer[...]


def stage(first, second, numer):
    state = jax.ShapeDtypeStruct((256, 512), F32)
    return pl.pallas_call(
        stage_kernel,
        in_specs=[VMEM] * 3,
        out_specs=[VMEM] * 3,
        out_shape=[state, state, jax.ShapeDtypeStruct((256, 512), BF16)],
        name="stage",
        **params_of(0, 2 << 20),
    )(first, second, numer)


def moments(shares, first, second):
    total = shares[0].astype(F32)
    for q in range(1, 4):
        total = total + shares[q].astype(F32)
    grad = total / 2048.0
    one = BETA_ONE * first[...] + (1.0 - BETA_ONE) * grad
    two = BETA_TWO * second[...] + (1.0 - BETA_TWO) * grad * grad
    return one, two


def adam_kernel(weight, bias, shares, first, second, numer, sent):
    one, two = moments(shares, first, second)
    update = LEARN * (one / bias[0]) / (jnp.sqrt(two / bias[1]) + EPSILON)
    sent[:256, :] = (numer[...].astype(F32) - update).astype(BF16)
    sent[256:, :] = jnp.full((16, 512), weight[0], F32).astype(BF16)


def adam(weight, bias, shares, first, second, numer):
    return pl.pallas_call(
        adam_kernel,
        in_specs=[SMEM, SMEM] + [VMEM] * 4,
        out_specs=VMEM,
        out_shape=jax.ShapeDtypeStruct((272, 512), BF16),
        name="adam",
        **params_of(0, 3 << 20),
    )(weight, bias, shares, first, second, numer)


def state_kernel(shares, first, second, new_first, new_second):
    new_first[...], new_second[...] = moments(shares, first, second)


def new_state(shares, first, second):
    state = jax.ShapeDtypeStruct((256, 512), F32)
    return pl.pallas_call(
        state_kernel,
        in_specs=[VMEM] * 3,
        out_specs=[VMEM] * 2,
        out_shape=[state, state],
        name="new_state",
        **params_of(0, 3 << 20),
    )(shares, first, second)


def combine_kernel(sent, incoming, new_params, mixed):
    new_params[...] = (
        (sent[:256, :].astype(F32) + incoming[:256, :].astype(F32)) * 0.5
    ).astype(BF16)
    mixed[0] = (
        jnp.max(sent[256:264, :128].astype(F32)) + jnp.max(incoming[256:264, :128].astype(F32))
    ) * 0.5


def combine(sent, incoming):
    return pl.pallas_call(
        combine_kernel,
        in_specs=[VMEM] * 2,
        out_specs=[VMEM, SMEM],
        out_shape=[jax.ShapeDtypeStruct((256, 512), BF16), jax.ShapeDtypeStruct((1,), F32)],
        name="combine",
        **params_of(0, COMBINE),
    )(sent, incoming)


def unpack_kernel(own, from_z, from_x, from_xz, token_grad, keys):
    place = lax.axis_index("xh") * 2 + lax.axis_index("zp")
    total = None
    for relative, part in enumerate((own, from_z, from_x, from_xz)):
        cls = place ^ relative
        for q in range(4):
            column = (cls // 2) * 2048 + q * 512 + (cls % 2) * 256
            token_grad[:, pl.ds(pl.multiple_of(column, 256), 256)] = part[:, q * 256 : (q + 1) * 256]
        term = part[:, 1024:].astype(F32)
        total = term if total is None else total + term
    keys[...] = total.astype(BF16)


def unpack(own, from_z, from_x, from_xz):
    return pl.pallas_call(
        unpack_kernel,
        in_specs=[VMEM] * 4,
        out_specs=[VMEM] * 2,
        out_shape=[jax.ShapeDtypeStruct((128, 4096), BF16), jax.ShapeDtypeStruct((128, 512), BF16)],
        name="unpack",
        **params_of(0, 3 << 20),
    )(own, from_z, from_x, from_xz)


def step_with(tokens, cotangent, params, first_moment, second_moment, weight, step, hop):
    mass = weight.astype(F32)
    tstep = step[0]
    count = (tstep + 1).astype(F32)
    bias = 1.0 - jnp.power(jnp.array([BETA_ONE, BETA_TWO], F32), count)

    numer = params[0]
    w_down = along_quad(numer, 1)
    w_up = along_quad(numer, -1)
    far = jnp.concatenate([along_quad(w_down[:128], 1), along_quad(w_up[128:], -1)], axis=0)
    rows = [numer, w_up, far, w_down]
    own, *sends = pack(tokens[0], cotangent[0])
    far_first = [swap_features(sends[r], r + 1) for r in (2, 1, 0)]
    blocks = [own] + far_first[::-1]
    mine, rows = lax.optimization_barrier((share(blocks), rows))
    shares = swap_tokens(mine)

    own, *sends = products(mass, blocks, rows)
    back = [swap_features(sends[r], r + 1) for r in (2, 1, 0)][::-1]

    first, second, base = stage(first_moment[0], second_moment[0], params[0])
    sent = adam(mass, bias, shares, first, second, base)
    incoming = pushed(sent, hop)
    shares, sent = lax.optimization_barrier((shares, sent))
    new_first, new_second = new_state(shares, first, second)
    new_params, mixed = combine(sent, incoming)
    own, new_first = lax.optimization_barrier((own, new_first))
    token_grad, keys = unpack(own, *back)
    return (
        keys[None],
        token_grad[None],
        new_params[None],
        new_first[None],
        new_second[None],
        mixed,
    )


def body(*args):
    branches = [partial(step_with, hop=2**level) for level in range(4)]
    return lax.switch(args[-1][0] & 3, branches, *args)


def solution(mesh):
    fine = Mesh(mesh.devices.reshape(8, 2, 2, 2, 4, 2), REPS + GROUP)
    rows = P(REPS, GROUP, None)
    return jax.shard_map(
        body,
        mesh=fine,
        in_specs=(rows, rows, rows, rows, rows, P(REPS), P()),
        out_specs=(rows, rows, rows, rows, rows, P(REPS)),
        check_vma=False,
    )
```

```python
from functools import partial

import jax
import jax.numpy as jnp
from jax import lax
from jax.experimental import pallas as pl
from jax.experimental.pallas import tpu as pltpu
from jax.sharding import Mesh, PartitionSpec as P

LEARN = 0.002
BETA_ONE = 0.9
BETA_TWO = 0.999
EPSILON = 1e-08
GROUP = ("xh", "zq", "zp")
REPS = ("y", "xl", "c")
PAIRS = ("c", "xh", "zq", "zp")
SHARE = 64 << 20
ADAM = 64 << 20
COMBINE = 64 << 20
F32 = jnp.float32
BF16 = jnp.bfloat16


def neighbour(core, z):
    return z ^ 1 if core == 0 else ((z + 1) ^ 1) - 1 & 7


def partner_pairs(relative):
    pairs = []
    for core in range(2):
        for xh in range(2):
            for z in range(8):
                to_z = neighbour(core, z) if relative & 1 else z
                to_x = xh ^ (relative >> 1)
                pairs.append((core * 16 + xh * 8 + z, core * 16 + to_x * 8 + to_z))
    return pairs


def along_quad(x, step):
    return lax.ppermute(x, "zq", [(i, (i + step) % 4) for i in range(4)])


def swap_tokens(x):
    return lax.all_to_all(x, "zq", 0, 0, tiled=True)


def swap_features(x, relative):
    return lax.ppermute(x, PAIRS, partner_pairs(relative))


def pushed(outgoing, hop):
    pairs = [(source, (source + hop) % 32) for source in range(32)]
    return lax.ppermute(outgoing, REPS, pairs)


VMEM = pl.BlockSpec(memory_space=pltpu.VMEM)
ANY = pl.BlockSpec(memory_space=pl.ANY)
SMEM = pl.BlockSpec(memory_space=pltpu.SMEM)


def params_of(flops=0, moved=0, mib=24):
    return dict(
        compiler_params=pltpu.CompilerParams(vmem_limit_bytes=mib << 20),
        cost_estimate=pl.CostEstimate(flops=flops, bytes_accessed=moved, transcendentals=0),
    )


def pack_kernel(tokens, cot, own, to_z, to_x, to_xz):
    place = lax.axis_index("xh") * 2 + lax.axis_index("zp")
    for relative, out in enumerate((own, to_z, to_x, to_xz)):
        cls = place ^ relative
        for q in range(4):
            column = (cls // 2) * 2048 + q * 512 + (cls % 2) * 256
            out[:, q * 256 : (q + 1) * 256] = tokens[:, pl.ds(pl.multiple_of(column, 256), 256)]
        out[:, 1024:] = cot[...]


def pack(tokens, cot):
    return pl.pallas_call(
        pack_kernel,
        in_specs=[VMEM] * 2,
        out_specs=[VMEM] * 4,
        out_shape=[jax.ShapeDtypeStruct((128, 1536), BF16)] * 4,
        name="pack",
        **params_of(0, 3 << 20),
    )(tokens, cot)


def share_kernel(t0, t1, t2, t3, c0, c1, c2, c3, out):
    total = None
    for tok, cot in ((t0, c0), (t1, c1), (t2, c2), (t3, c3)):
        term = lax.dot_general(
            tok[...], cot[...], (((0,), (0,)), ((), ())), preferred_element_type=F32
        )
        total = term if total is None else total + term
    out[0] = total.astype(BF16)


def share(blocks):
    return pl.pallas_call(
        share_kernel,
        grid=(4,),
        in_specs=[pl.BlockSpec((128, 256), lambda q: (0, q))] * 4
        + [pl.BlockSpec((128, 512), lambda q: (0, 2))] * 4,
        out_specs=pl.BlockSpec((1, 256, 512), lambda q: (q, 0, 0)),
        out_shape=pltpu.HBM((4, 256, 512), BF16),
        name="share",
        **params_of(0, SHARE),
    )(*blocks, *blocks)


def product_kernel(weight, b0, b1, b2, b3, w0, w1, w2, w3, own, to_z, to_x, to_xz, got):
    quad = lax.axis_index("zq")
    for k, block in enumerate((b0, b1, b2, b3)):
        got[k * 128 : (k + 1) * 128, :] = block[...]
    outs = (own, to_z, to_x, to_xz)
    cot = got[:, 1024:]
    keys = None
    for q, w in enumerate((w0, w1, w2, w3)):
        columns = pl.ds(pl.multiple_of(lax.rem(quad + q, 4) * 256, 256), 256)
        w = (w[...].astype(F32) / weight[0]).astype(BF16)
        term = jnp.dot(got[:, columns], w, preferred_element_type=F32)
        keys = term if keys is None else keys + term
        part = lax.dot_general(
            cot, w, (((1,), (1,)), ((), ())), preferred_element_type=F32
        ).astype(BF16)
        for k, out in enumerate(outs):
            out[:, columns] = part[k * 128 : (k + 1) * 128, :]
    keys = keys.astype(BF16)
    for k, out in enumerate(outs):
        out[:, 1024:] = keys[k * 128 : (k + 1) * 128, :]


def products(weight, blocks, w):
    block = jax.ShapeDtypeStruct((128, 1536), BF16)
    return pl.pallas_call(
        product_kernel,
        in_specs=[SMEM] + [VMEM] * 8,
        out_specs=[VMEM] * 4,
        out_shape=[block] * 4,
        scratch_shapes=[pltpu.VMEM((512, 1536), BF16)],
        name="products",
        **params_of(4 * 512 * 1024 * 512, 4 << 20),
    )(weight, *blocks, *w)


def adam_kernel(weight, bias, shares, first, second, numer, new_first, new_second, sent):
    total = shares[0].astype(F32)
    for q in range(1, 4):
        total = total + shares[q].astype(F32)
    grad = total / 2048.0
    one = BETA_ONE * first[...] + (1.0 - BETA_ONE) * grad
    two = BETA_TWO * second[...] + (1.0 - BETA_TWO) * grad * grad
    new_first[...] = one
    new_second[...] = two
    update = LEARN * (one / bias[0]) / (jnp.sqrt(two / bias[1]) + EPSILON)
    sent[:256, :] = (numer[...].astype(F32) - update).astype(BF16)
    sent[256:, :] = jnp.full((16, 512), weight[0], F32).astype(BF16)


def adam(weight, bias, shares, first, second, numer):
    state = jax.ShapeDtypeStruct((256, 512), F32)
    return pl.pallas_call(
        adam_kernel,
        in_specs=[SMEM, SMEM] + [VMEM] * 4,
        out_specs=[VMEM] * 3,
        out_shape=[state, state, jax.ShapeDtypeStruct((272, 512), BF16)],
        name="adam",
        **params_of(0, ADAM),
    )(weight, bias, shares, first, second, numer)


def combine_kernel(sent, incoming, new_params, mixed):
    new_params[...] = (
        (sent[:256, :].astype(F32) + incoming[:256, :].astype(F32)) * 0.5
    ).astype(BF16)
    mixed[0] = (
        jnp.max(sent[256:264, :128].astype(F32)) + jnp.max(incoming[256:264, :128].astype(F32))
    ) * 0.5


def combine(sent, incoming):
    return pl.pallas_call(
        combine_kernel,
        in_specs=[VMEM] * 2,
        out_specs=[VMEM, SMEM],
        out_shape=[jax.ShapeDtypeStruct((256, 512), BF16), jax.ShapeDtypeStruct((1,), F32)],
        name="combine",
        **params_of(0, COMBINE),
    )(sent, incoming)


def unpack_kernel(own, from_z, from_x, from_xz, token_grad, keys):
    place = lax.axis_index("xh") * 2 + lax.axis_index("zp")
    total = None
    for relative, part in enumerate((own, from_z, from_x, from_xz)):
        cls = place ^ relative
        for q in range(4):
            column = (cls // 2) * 2048 + q * 512 + (cls % 2) * 256
            token_grad[:, pl.ds(pl.multiple_of(column, 256), 256)] = part[:, q * 256 : (q + 1) * 256]
        term = part[:, 1024:].astype(F32)
        total = term if total is None else total + term
    keys[...] = total.astype(BF16)


def unpack(own, from_z, from_x, from_xz):
    return pl.pallas_call(
        unpack_kernel,
        in_specs=[VMEM] * 4,
        out_specs=[VMEM] * 2,
        out_shape=[jax.ShapeDtypeStruct((128, 4096), BF16), jax.ShapeDtypeStruct((128, 512), BF16)],
        name="unpack",
        **params_of(0, 3 << 20),
    )(own, from_z, from_x, from_xz)


def step_with(tokens, cotangent, params, first_moment, second_moment, weight, step, hop):
    mass = weight.astype(F32)
    tstep = step[0]
    count = (tstep + 1).astype(F32)
    bias = 1.0 - jnp.power(jnp.array([BETA_ONE, BETA_TWO], F32), count)

    numer = params[0]
    w_down = along_quad(numer, 1)
    w_up = along_quad(numer, -1)
    far = jnp.concatenate([along_quad(w_down[:128], 1), along_quad(w_up[128:], -1)], axis=0)
    rows = [numer, w_up, far, w_down]
    own, *sends = pack(tokens[0], cotangent[0])
    blocks = [own] + [swap_features(x, r + 1) for r, x in enumerate(sends)]
    rows, blocks = lax.optimization_barrier((rows, blocks))
    shares = swap_tokens(share(blocks))

    own, *sends = products(mass, blocks, rows)
    back = [swap_features(x, r + 1) for r, x in enumerate(sends)]

    new_first, new_second, sent = adam(
        mass, bias, shares, first_moment[0], second_moment[0], params[0]
    )
    incoming = pushed(sent, hop)
    new_params, mixed = combine(sent, incoming)
    token_grad, keys = unpack(own, *back)
    return (
        keys[None],
        token_grad[None],
        new_params[None],
        new_first[None],
        new_second[None],
        mixed,
    )


def body(*args):
    branches = [partial(step_with, hop=2**level) for level in range(4)]
    return lax.switch(args[-1][0] & 3, branches, *args)


def solution(mesh):
    fine = Mesh(mesh.devices.reshape(8, 2, 2, 2, 4, 2), REPS + GROUP)
    rows = P(REPS, GROUP, None)
    return jax.shard_map(
        body,
        mesh=fine,
        in_specs=(rows, rows, rows, rows, rows, P(REPS), P()),
        out_specs=(rows, rows, rows, rows, rows, P(REPS)),
        check_vma=False,
    )
```

```python
from functools import partial

import jax
import jax.numpy as jnp
from jax import lax
from jax.experimental import pallas as pl
from jax.experimental.pallas import tpu as pltpu
from jax.sharding import Mesh, PartitionSpec as P

LEARN = 0.002
BETA_ONE = 0.9
BETA_TWO = 0.999
EPSILON = 1e-08
GROUP = ("xh", "zq", "zp")
REPS = ("y", "xl", "c")
PAIRS = ("c", "xh", "zq", "zp")
SHARE = 64 << 20
ADAM = 64 << 20
COMBINE = 64 << 20
F32 = jnp.float32
BF16 = jnp.bfloat16


def neighbour(core, z):
    return z ^ 1 if core == 0 else ((z + 1) ^ 1) - 1 & 7


def partner_pairs(relative):
    pairs = []
    for core in range(2):
        for xh in range(2):
            for z in range(8):
                to_z = neighbour(core, z) if relative & 1 else z
                to_x = xh ^ (relative >> 1)
                pairs.append((core * 16 + xh * 8 + z, core * 16 + to_x * 8 + to_z))
    return pairs


def along_quad(x, step):
    return lax.ppermute(x, "zq", [(i, (i + step) % 4) for i in range(4)])


def swap_tokens(x):
    return lax.all_to_all(x, "zq", 0, 0, tiled=True)


def swap_features(x, relative):
    return lax.ppermute(x, PAIRS, partner_pairs(relative))


def pushed(outgoing, hop):
    pairs = [(source, (source + hop) % 32) for source in range(32)]
    return lax.ppermute(outgoing, REPS, pairs)


VMEM = pl.BlockSpec(memory_space=pltpu.VMEM)
ANY = pl.BlockSpec(memory_space=pl.ANY)
SMEM = pl.BlockSpec(memory_space=pltpu.SMEM)


def params_of(flops=0, moved=0, mib=24):
    return dict(
        compiler_params=pltpu.CompilerParams(vmem_limit_bytes=mib << 20),
        cost_estimate=pl.CostEstimate(flops=flops, bytes_accessed=moved, transcendentals=0),
    )


def pack_kernel(tokens, cot, own, to_z, to_x, to_xz):
    place = lax.axis_index("xh") * 2 + lax.axis_index("zp")
    for relative, out in enumerate((own, to_z, to_x, to_xz)):
        cls = place ^ relative
        for q in range(4):
            column = (cls // 2) * 2048 + q * 512 + (cls % 2) * 256
            out[:, q * 256 : (q + 1) * 256] = tokens[:, pl.ds(pl.multiple_of(column, 256), 256)]
        out[:, 1024:] = cot[...]


def pack(tokens, cot):
    return pl.pallas_call(
        pack_kernel,
        in_specs=[VMEM] * 2,
        out_specs=[VMEM] * 4,
        out_shape=[jax.ShapeDtypeStruct((128, 1536), BF16)] * 4,
        name="pack",
        **params_of(0, 3 << 20),
    )(tokens, cot)


def share_kernel(t0, t1, t2, t3, c0, c1, c2, c3, out):
    total = None
    for tok, cot in ((t0, c0), (t1, c1), (t2, c2), (t3, c3)):
        term = lax.dot_general(
            tok[...], cot[...], (((0,), (0,)), ((), ())), preferred_element_type=F32
        )
        total = term if total is None else total + term
    out[0] = total.astype(BF16)


def share(blocks):
    return pl.pallas_call(
        share_kernel,
        grid=(4,),
        in_specs=[pl.BlockSpec((128, 256), lambda q: (0, q))] * 4
        + [pl.BlockSpec((128, 512), lambda q: (0, 2))] * 4,
        out_specs=pl.BlockSpec((1, 256, 512), lambda q: (q, 0, 0)),
        out_shape=pltpu.HBM((4, 256, 512), BF16),
        name="share",
        **params_of(0, SHARE),
    )(*blocks, *blocks)


def product_kernel(weight, b0, b1, b2, b3, w0, w1, w2, w3, own, to_z, to_x, to_xz, got):
    quad = lax.axis_index("zq")
    for k, block in enumerate((b0, b1, b2, b3)):
        got[k * 128 : (k + 1) * 128, :] = block[...]
    outs = (own, to_z, to_x, to_xz)
    cot = got[:, 1024:]
    keys = None
    for q, w in enumerate((w0, w1, w2, w3)):
        columns = pl.ds(pl.multiple_of(lax.rem(quad + q, 4) * 256, 256), 256)
        w = (w[...].astype(F32) / weight[0]).astype(BF16)
        term = jnp.dot(got[:, columns], w, preferred_element_type=F32)
        keys = term if keys is None else keys + term
        part = lax.dot_general(
            cot, w, (((1,), (1,)), ((), ())), preferred_element_type=F32
        ).astype(BF16)
        for k, out in enumerate(outs):
            out[:, columns] = part[k * 128 : (k + 1) * 128, :]
    keys = keys.astype(BF16)
    for k, out in enumerate(outs):
        out[:, 1024:] = keys[k * 128 : (k + 1) * 128, :]


def products(weight, blocks, w):
    block = jax.ShapeDtypeStruct((128, 1536), BF16)
    return pl.pallas_call(
        product_kernel,
        in_specs=[SMEM] + [VMEM] * 8,
        out_specs=[VMEM] * 4,
        out_shape=[block] * 4,
        scratch_shapes=[pltpu.VMEM((512, 1536), BF16)],
        name="products",
        **params_of(4 * 512 * 1024 * 512, 4 << 20),
    )(weight, *blocks, *w)


def moments(shares, first, second):
    total = shares[0].astype(F32)
    for q in range(1, 4):
        total = total + shares[q].astype(F32)
    grad = total / 2048.0
    one = BETA_ONE * first[...] + (1.0 - BETA_ONE) * grad
    two = BETA_TWO * second[...] + (1.0 - BETA_TWO) * grad * grad
    return one, two


def adam_kernel(weight, bias, shares, first, second, numer, sent):
    one, two = moments(shares, first, second)
    update = LEARN * (one / bias[0]) / (jnp.sqrt(two / bias[1]) + EPSILON)
    sent[:256, :] = (numer[...].astype(F32) - update).astype(BF16)
    sent[256:, :] = jnp.full((16, 512), weight[0], F32).astype(BF16)


def adam(weight, bias, shares, first, second, numer):
    return pl.pallas_call(
        adam_kernel,
        in_specs=[SMEM, SMEM] + [VMEM] * 4,
        out_specs=VMEM,
        out_shape=jax.ShapeDtypeStruct((272, 512), BF16),
        name="adam",
        **params_of(0, 3 << 20),
    )(weight, bias, shares, first, second, numer)


def state_kernel(shares, first, second, new_first, new_second):
    new_first[...], new_second[...] = moments(shares, first, second)


def new_state(shares, first, second):
    state = jax.ShapeDtypeStruct((256, 512), F32)
    return pl.pallas_call(
        state_kernel,
        in_specs=[VMEM] * 3,
        out_specs=[VMEM] * 2,
        out_shape=[state, state],
        name="new_state",
        **params_of(0, 3 << 20),
    )(shares, first, second)


def combine_kernel(sent, incoming, new_params, mixed):
    new_params[...] = (
        (sent[:256, :].astype(F32) + incoming[:256, :].astype(F32)) * 0.5
    ).astype(BF16)
    mixed[0] = (
        jnp.max(sent[256:264, :128].astype(F32)) + jnp.max(incoming[256:264, :128].astype(F32))
    ) * 0.5


def combine(sent, incoming):
    return pl.pallas_call(
        combine_kernel,
        in_specs=[VMEM] * 2,
        out_specs=[VMEM, SMEM],
        out_shape=[jax.ShapeDtypeStruct((256, 512), BF16), jax.ShapeDtypeStruct((1,), F32)],
        name="combine",
        **params_of(0, COMBINE),
    )(sent, incoming)


def unpack_kernel(own, from_z, from_x, from_xz, token_grad, keys):
    place = lax.axis_index("xh") * 2 + lax.axis_index("zp")
    total = None
    for relative, part in enumerate((own, from_z, from_x, from_xz)):
        cls = place ^ relative
        for q in range(4):
            column = (cls // 2) * 2048 + q * 512 + (cls % 2) * 256
            token_grad[:, pl.ds(pl.multiple_of(column, 256), 256)] = part[:, q * 256 : (q + 1) * 256]
        term = part[:, 1024:].astype(F32)
        total = term if total is None else total + term
    keys[...] = total.astype(BF16)


def unpack(own, from_z, from_x, from_xz):
    return pl.pallas_call(
        unpack_kernel,
        in_specs=[VMEM] * 4,
        out_specs=[VMEM] * 2,
        out_shape=[jax.ShapeDtypeStruct((128, 4096), BF16), jax.ShapeDtypeStruct((128, 512), BF16)],
        name="unpack",
        **params_of(0, 3 << 20),
    )(own, from_z, from_x, from_xz)


def step_with(tokens, cotangent, params, first_moment, second_moment, weight, step, hop):
    mass = weight.astype(F32)
    tstep = step[0]
    count = (tstep + 1).astype(F32)
    bias = 1.0 - jnp.power(jnp.array([BETA_ONE, BETA_TWO], F32), count)

    numer = params[0]
    w_down = along_quad(numer, 1)
    w_up = along_quad(numer, -1)
    far = jnp.concatenate([along_quad(w_down[:128], 1), along_quad(w_up[128:], -1)], axis=0)
    rows = [numer, w_up, far, w_down]
    own, *sends = pack(tokens[0], cotangent[0])
    blocks = [own] + [swap_features(x, r + 1) for r, x in enumerate(sends)]
    mine, rows = lax.optimization_barrier((share(blocks), rows))
    shares = swap_tokens(mine)

    own, *sends = products(mass, blocks, rows)
    back = [swap_features(x, r + 1) for r, x in enumerate(sends)]

    first, second = first_moment[0], second_moment[0]
    sent = adam(mass, bias, shares, first, second, params[0])
    incoming = pushed(sent, hop)
    shares, sent = lax.optimization_barrier((shares, sent))
    new_first, new_second = new_state(shares, first, second)
    new_params, mixed = combine(sent, incoming)
    token_grad, keys = unpack(own, *back)
    return (
        keys[None],
        token_grad[None],
        new_params[None],
        new_first[None],
        new_second[None],
        mixed,
    )


def body(*args):
    branches = [partial(step_with, hop=2**level) for level in range(4)]
    return lax.switch(args[-1][0] & 3, branches, *args)


def solution(mesh):
    fine = Mesh(mesh.devices.reshape(8, 2, 2, 2, 4, 2), REPS + GROUP)
    rows = P(REPS, GROUP, None)
    return jax.shard_map(
        body,
        mesh=fine,
        in_specs=(rows, rows, rows, rows, rows, P(REPS), P()),
        out_specs=(rows, rows, rows, rows, rows, P(REPS)),
        check_vma=False,
    )
```
